256 devices in a mesh: section: 4 (over z_lo, core), ctx: 16 (over x, y), tp: 4 (over z_hi).
Axes of the slice: x: 4, y: 4, z: 8 (z_hi: 4, z_lo: 2; z = z_hi * 2 + z_lo), core: 2. Of those that a mesh axis runs over, the one named last changes fastest.
Arguments:
- layer_inputs: bfloat16 [4, 16384, 5120], P('section', 'ctx', 'tp'), may hold values from -6 to 6
- norm_gain: bfloat16 [4, 5120], P('section', 'tp'), may hold values from 0.25 to 1.75
- kv_weight: bfloat16 [4, 5120, 2048], P('section', None, 'tp'), may hold values from -0.078125 to 0.078125
- span_pages: int32 [4], replicated, may hold values from 1 to 512, 1024 in all
- page_owner: int32 [1024, 1], replicated, may hold values from 0 to 15; in each aligned block of 64 rows (0 to 63, 64 to 127, ...) at most 8 rows name the same one
- cache_len: int32 [4], replicated, may hold values from 1 to 8192
- cache_kv: bfloat16 [4, 4, 8192, 2048], P('section', None, 'ctx', 'tp'), may hold values from -6 to 6
- queries: bfloat16 [4, 4, 4, 4096], P('section', None, None, 'tp'), may hold values from -150 to 150
- new_kv: bfloat16 [4, 4, 4, 2048], P('section', None, None, 'tp'), may hold values from -6 to 6
Outputs:
- page_store: bfloat16 [4, 2048, 16, 2048], P('section', 'ctx', None, 'tp')
- attention: bfloat16 [4, 4, 4, 4096], P('section', None, None, 'tp')
The draws below stay inside these ranges and needn't reach their ends.
All inputs are finite; a program needn't handle non-finite values.
Results may differ from the reference program's by a relative error of at most 0.013.
Values may be sent and summed in bfloat16 or wider, within the bound.
No kernel may reach another device: no remote copies, remote signals or barrier semaphores. Data moves between devices by JAX's collectives and lax.ppermute only.
A program may use at most 128 MiB of HBM per device.

```python
import math
import jax
import jax.numpy as jnp
import numpy as np
from jax import lax

D = 5120
HEADS = 32
KV_HEADS = 8
HEAD_DIM = 128
SESSIONS = 4
STEPS = 4
PAGE = 16
PAGES_DEV = 64
LAYERS = 4
PAGES = 1024
ROWS = 16384
CONTEXT = 8192
CAPACITY = 8
MOST_PG = 512
KV_COLS = 2048
N_SECTION = 4
N_CTX = 16
N_TP = 4


def draw_cache_len(key, part):
    key = jax.random.fold_in(key, 11)
    first, second = jax.random.split(key)
    lengths = jax.random.randint(first, (SESSIONS,), 1, CONTEXT + 1)
    chosen = jax.random.randint(second, (), 0, SESSIONS)
    return jnp.where(jnp.arange(SESSIONS) == chosen, CONTEXT, lengths).astype(jnp.int32)


def draw_queries(key, part):
    key = jax.random.fold_in(key, 23)
    first, second = jax.random.split(key)
    base = jnp.clip(jax.random.normal(first, (LAYERS, SESSIONS, STEPS, HEADS * HEAD_DIM), jnp.float32), -5.0, 5.0)
    scale = jnp.exp(jax.random.uniform(second, (LAYERS, SESSIONS, STEPS, 1), jnp.float32, 0.0, 0.7))
    return (base * scale).astype(jnp.bfloat16)


def block_levels(rng, shape, shards, least, top_value):
    def one(dim, parts):
        draws = jax.random.uniform(jax.random.fold_in(jax.random.fold_in(rng, 6), dim), (parts,), jnp.float32, least / len(shards), top_value / len(shards))
        return jnp.repeat(jnp.exp(draws), shape[dim] // parts).reshape((-1,) + (1,) * (len(shape) - dim - 1))

    loudness = one(*shards[0])
    for cut in shards[1:]:
        loudness = loudness * one(*cut)
    return loudness


def length_profile(count, total, bound, skew):
    weights = [(1 << 20) // math.isqrt(grade ** skew) + 1 for grade in range(2, count + 1)]
    spare, counts = total - bound - (count - 1), [1] * (count - 1)
    while spare > 0:
        movable = [i for i in range(count - 1) if counts[i] < bound]
        pool, budget = sum([weights[i] for i in movable]), spare
        for i in movable:
            more = min(bound - counts[i], max(1, budget * weights[i] // pool), spare)
            counts[i] = counts[i] + more
            spare = spare - more
    return np.array([bound] + counts)


def ragged(stream_key, amount, total, limit, skew):
    if amount == 2:
        one = jax.random.randint(stream_key, (), max(1, total - limit), min(limit, total - 1) + 1)
        return jnp.stack([one, total - one])
    tallies = jnp.asarray(length_profile(amount, total, limit, skew), jnp.int32)
    pairs = (amount - 1) // 2
    source_of, sink = tallies[1:1 + 2 * pairs:2], tallies[2:2 + 2 * pairs:2]
    slack = jnp.minimum(source_of - 1, limit - sink)
    passed = jax.random.randint(jax.random.fold_in(stream_key, 1), (pairs,), 0, 1 << 20) % (slack + 1)
    tallies = tallies.at[1:1 + 2 * pairs:2].set(source_of - passed).at[2:2 + 2 * pairs:2].set(sink + passed)
    return tallies[jax.random.permutation(jax.random.fold_in(stream_key, 2), amount)]


def shared_out(stream_key, own, number, rows, amount, top, most, lean):
    sequence = jax.random.permutation(stream_key, amount)
    heavy_load, ordinary = shares(amount, rows * top, most, lean, True), shares(amount, rows * top, most, lean, False)
    places = jnp.arange(amount)

    def named(tallies, offset_by):
        used = int((tallies > 0).sum())
        fixed = max(1, used // 4)
        shifted = fixed + (places - fixed + offset_by * (used - fixed)) % max(1, amount - fixed)
        return jnp.zeros((amount,), jnp.int32).at[sequence[jnp.where(places < fixed, places, shifted)]].set(jnp.asarray(tallies, jnp.int32))

    tallies = jnp.where(number % 4 == 0, named(heavy_load, number // 4), named(ordinary, number - number // 4 - 1))
    mixed = jax.random.permutation(jax.random.fold_in(own, 3), amount)
    giver, sink = mixed[0:amount // 2 * 2:2], mixed[1:amount // 2 * 2:2]
    margin = jnp.minimum(tallies[giver] - 1, most - tallies[sink]) // 2
    margin = jnp.where((giver == sequence[0]) | (sink == sequence[0]) | (tallies[sink] == 0), 0, jnp.maximum(margin, 0))
    shifted = jax.random.randint(jax.random.fold_in(own, 4), (amount // 2,), 0, 1 << 20) % (margin + 1)
    tallies = tallies.at[giver].add(-shifted).at[sink].add(shifted)
    members = jnp.searchsorted(jnp.cumsum(tallies), jnp.arange(rows * top), side="right").astype(jnp.int32)
    table = members.reshape(top, rows).T
    table = table[jax.random.permutation(jax.random.fold_in(own, 1), rows)]
    offset_by = jax.random.randint(jax.random.fold_in(own, 2), (rows, 1), 0, top)
    return jnp.take_along_axis(table, (jnp.arange(top)[None, :] + offset_by) % top, axis=1)


def shares(number_of, total, bound, skew, full):
    weights = [(1 << 20) // math.isqrt(rank ** skew) + 1 for rank in range(1, number_of + 1)]
    largest = bound if full else min(bound, max(-(-total // number_of), total * weights[0] // sum(weights)))
    least = 1 if total - largest >= number_of - 1 else 0
    holding, surplus = [largest] + [least] * (number_of - 1), total - largest - least * (number_of - 1)
    while surplus > 0:
        movable = [i for i in range(1, number_of) if holding[i] < largest] or [i for i in range(1, number_of) if holding[i] < bound]
        whole, left = sum([weights[i] for i in movable]), surplus
        for i in movable:
            more = min(bound - holding[i], max(1, left * weights[i] // whole), surplus)
            holding[i] = holding[i] + more
            surplus = surplus - more
    return np.array(holding)


def normal_values(key, extent, width, reach, shards=(), held_as=jnp.bfloat16):
    entries = jax.random.normal(key, extent, jnp.float32) * width
    if len(shards) > 0:
        entries = block_levels(key, extent, shards, -0.22, 0.18) * entries
    return jnp.clip(entries, min=-reach, max=reach).astype(held_as)


def setup_inputs(seed: int = 0) -> dict:
    key_list = jax.random.split(jax.random.key(seed), 10)
    layer_inputs = normal_values(key_list[0], (LAYERS, ROWS, D), 1.0, 6.0, ((0, 4), (1, 16), (2, 4)))
    norm_gain = jnp.clip(1.0 + 0.15 * jax.random.normal(key_list[1], (LAYERS, D), jnp.float32), 0.25, 1.75).astype(jnp.bfloat16)
    kv_weight = normal_values(key_list[2], (LAYERS, D, KV_COLS), D ** -0.5, 0.078125, ((0, 4), (2, 4)))
    span_pages = ragged(key_list[3], SESSIONS, PAGES, MOST_PG, 2).astype(jnp.int32)
    page_owner_keys = jax.random.split(jax.random.fold_in(key_list[4], 1), PAGES // PAGES_DEV)
    page_owner_turns = jax.random.permutation(jax.random.fold_in(key_list[4], 3), PAGES // PAGES_DEV)
    page_owner = jax.vmap(lambda own, number: shared_out(jax.random.fold_in(key_list[4], 2), own, number, PAGES_DEV, N_CTX, 1, CAPACITY, 2))(page_owner_keys, page_owner_turns).reshape((PAGES, 1))
    cache_len = draw_cache_len(jax.random.fold_in(key_list[9], 71), 0)
    cache_kv = normal_values(key_list[6], (LAYERS, SESSIONS, CONTEXT, KV_COLS), 1.0, 6.0, ((0, 4), (2, 16), (3, 4)))
    queries = draw_queries(jax.random.fold_in(key_list[9], 71), 0)
    new_kv = normal_values(key_list[8], (LAYERS, SESSIONS, STEPS, KV_COLS), 1.0, 6.0, ((0, 4), (3, 4)))
    return dict(layer_inputs=layer_inputs, norm_gain=norm_gain, kv_weight=kv_weight, span_pages=span_pages, page_owner=page_owner, cache_len=cache_len, cache_kv=cache_kv, queries=queries, new_kv=new_kv)


epsilon = 1e-05

def split_pairs(block, groups, per_group):
    shaped = block.reshape(block.shape[:-1] + (groups, 2, per_group, HEAD_DIM))
    lead = block.shape[:-1] + (groups * per_group, HEAD_DIM)
    return (shaped[..., 0, :, :].reshape(lead), shaped[..., 1, :, :].reshape(lead))

def page_tables(span_pages, page_owner):
    total_pages = PAGES_DEV * N_CTX
    capacity = max(2, 2 * PAGES_DEV // N_CTX)
    page_index = jnp.arange(total_pages, dtype=jnp.int32)
    ends = jnp.cumsum(span_pages)
    session_of = lax.optimization_barrier(jnp.sum((ends[None, :] <= page_index[:, None]).astype(jnp.int32), axis=1))
    owner = page_owner[:, 0]
    onehot = (owner[:, None] == jnp.arange(N_CTX, dtype=jnp.int32)[None, :]).astype(jnp.int32)
    running = jnp.cumsum(onehot.reshape(N_CTX, PAGES_DEV, N_CTX), axis=1).reshape(total_pages, N_CTX)
    rank = lax.optimization_barrier(jnp.sum((running - 1) * onehot, axis=1))
    slot = owner * (N_CTX * capacity) + page_index // PAGES_DEV * capacity + rank
    return (session_of, slot.astype(jnp.int32), capacity)

def decode_layer(query, cache, cache_len, page_rows, row_session, new_block):
    per_group = KV_HEADS // N_TP
    group = HEADS // KV_HEADS
    page_keys, page_values = split_pairs(page_rows, N_TP, per_group)
    page_keys = page_keys.astype(jnp.float32)
    page_values = page_values.astype(jnp.float32)
    positions = jnp.arange(CONTEXT, dtype=jnp.int32)
    causal = jnp.arange(STEPS)[None, :] <= jnp.arange(STEPS)[:, None]

    def one_session(items):
        query_rows, cache_rows, length, session, fresh = items
        heads = query_rows.astype(jnp.float32).reshape(STEPS, KV_HEADS, group, HEAD_DIM)
        cache_keys, cache_values = split_pairs(cache_rows, N_TP, per_group)
        new_keys, new_values = split_pairs(fresh, N_TP, per_group)
        keys = jnp.concatenate([cache_keys.astype(jnp.float32), page_keys, new_keys.astype(jnp.float32)], 0)
        values = jnp.concatenate([cache_values.astype(jnp.float32), page_values, new_values.astype(jnp.float32)], 0)
        base = jnp.concatenate([positions < length, row_session == session], 0)
        allowed = jnp.concatenate([jnp.broadcast_to(base[None, :], (STEPS, base.shape[0])), causal], 1)
        scores = jnp.einsum('tkge,lke->tkgl', heads, keys, precision=lax.Precision.HIGHEST) * HEAD_DIM ** (-0.5)
        mask = allowed[:, None, None, :]
        peak = lax.optimization_barrier(jnp.max(jnp.where(mask, scores, -jnp.inf), axis=-1, keepdims=True))
        weights = jnp.where(mask, jnp.exp(scores - peak), 0.0)
        total = lax.optimization_barrier(jnp.sum(weights, axis=-1))
        mixed = jnp.einsum('tkgl,lke->tkge', weights, values, precision=lax.Precision.HIGHEST) / total[..., None]
        return mixed.reshape(STEPS, HEADS * HEAD_DIM).astype(jnp.bfloat16)
    sessions = jnp.arange(SESSIONS, dtype=jnp.int32)
    return lax.map(one_session, (query, cache, cache_len, sessions, new_block))

def reference(layer_inputs, norm_gain, kv_weight, span_pages, page_owner, cache_len, cache_kv, queries, new_kv):
    session_of, slot, capacity = page_tables(span_pages, page_owner)
    row_session = jnp.repeat(session_of, PAGE)
    kv_cols = 2 * KV_HEADS * HEAD_DIM
    hidden = layer_inputs[0]
    stores = []
    outputs = []
    for layer in range(N_SECTION):
        if layer > 0:
            hidden = (hidden.astype(jnp.float32) + layer_inputs[layer].astype(jnp.float32)).astype(jnp.bfloat16)
        wide = hidden.astype(jnp.float32)
        mean_sq = lax.optimization_barrier(jnp.mean(wide * wide, axis=1, keepdims=True))
        normed = (wide * lax.rsqrt(mean_sq + epsilon) * norm_gain[layer].astype(jnp.float32)).astype(jnp.bfloat16)
        fresh = jnp.dot(normed, kv_weight[layer], preferred_element_type=jnp.float32).astype(jnp.bfloat16)
        paged = fresh.reshape(PAGES_DEV * N_CTX, PAGE, kv_cols)
        store = jnp.zeros((N_CTX * N_CTX * capacity, PAGE, kv_cols), jnp.bfloat16).at[slot].set(paged)
        stores.append(store)
        outputs.append(decode_layer(queries[layer], cache_kv[layer], cache_len, fresh, row_session, new_kv[layer]))
    return (jnp.stack(stores), jnp.stack(outputs))
```

```python
import functools

import jax
import jax.numpy as jnp
from jax import lax
from jax.experimental import pallas as pl
from jax.experimental.pallas import tpu as pltpu
from jax.sharding import PartitionSpec as P

D = 5120
HEAD_DIM = 128
SESSIONS = 4
STEPS = 4
PAGE = 16
SIDE = 4

epsilon = 1e-05
floor_value = -1e30
bf16 = jnp.bfloat16
f32 = jnp.float32
VMEM = pl.BlockSpec(memory_space=pltpu.VMEM)
SMEM = pl.BlockSpec(memory_space=pltpu.SMEM)
ANY = pl.BlockSpec(memory_space=pl.ANY)
MEBI = 1024 * 1024
NO_COST = pl.CostEstimate(flops=0, bytes_accessed=0, transcendentals=0)


def shift_tp(array, by):
    peers = lax.axis_size("tp")
    return lax.ppermute(array, "tp", [(i, (i + by) % peers) for i in range(peers)])


def from_x(array, by):
    pairs = [(((i // SIDE + by) % SIDE) * SIDE + i % SIDE, i) for i in range(SIDE * SIDE)]
    return lax.ppermute(array, "ctx", pairs)


def from_y(array, by):
    pairs = [((i // SIDE) * SIDE + (i % SIDE + by) % SIDE, i) for i in range(SIDE * SIDE)]
    return lax.ppermute(array, "ctx", pairs)


def added(first, second):
    return (first.astype(f32) + second.astype(f32)).astype(bf16)


def add_kernel(first, second, *refs):
    refs[-1][...] = added(first[...], second[...])


def add_after(first, second, *after):
    rows, columns = first.shape
    block = pl.BlockSpec((rows // 4, columns), lambda i: (i, 0))
    return pl.pallas_call(
        add_kernel,
        grid=(4,),
        out_shape=jax.ShapeDtypeStruct(first.shape, bf16),
        in_specs=[block, block] + [ANY] * len(after),
        out_specs=block,
        compiler_params=pltpu.CompilerParams(vmem_limit_bytes=8 * MEBI),
        cost_estimate=NO_COST,
    )(first, second, *after)


def nothing(*refs):
    pass


def tied(array, *after):
    return pl.pallas_call(
        nothing,
        out_shape=jax.ShapeDtypeStruct(array.shape, array.dtype),
        in_specs=[ANY] * (1 + len(after)),
        out_specs=ANY,
        input_output_aliases={0: 0},
        cost_estimate=NO_COST,
    )(array, *after)


def pieces_kernel(place, weight, one, three, far, sems):
    x, y, rank = place[0], place[1], place[2]
    rows = one.shape[0]
    features = rows * SIDE
    copies = []
    for n, (out, behind, row, column) in enumerate(((one, 1, y, x), (three, 3, y, x), (far, 2, x, y))):
        start = lax.rem(rank + SIDE - behind, SIDE) * features + row * rows
        copies.append(
            pltpu.make_async_copy(
                weight.at[
                    pl.ds(pl.multiple_of(start, rows), rows),
                    pl.ds(pl.multiple_of(column * HEAD_DIM, HEAD_DIM), HEAD_DIM),
                ],
                out,
                sems.at[n],
            )
        )
    for copy in copies:
        copy.start()
    for copy in copies:
        copy.wait()


def rows_kernel(axis, place, *refs):
    out = refs[-1]
    rows = refs[0].shape[-2]
    for k in range(SIDE):
        start = pl.multiple_of(lax.rem(place[axis] + k, SIDE) * rows, rows)
        if len(out.shape) == 2:
            out[pl.ds(start, rows), :] = refs[k][...]
        else:
            out[:, pl.ds(start, rows), :] = refs[k][...]


def columns_kernel(place, *refs):
    out = refs[-1]
    half = out.shape[1] // 2
    for k in range(SIDE):
        start = lax.rem(place[0] + k, SIDE) * HEAD_DIM
        for n in range(2):
            out[:, pl.ds(pl.multiple_of(n * half + start, HEAD_DIM), HEAD_DIM)] = refs[k][n]


def dot_rows(hs, weight, start):
    return jnp.dot(hs[start : start + 256, :], weight, preferred_element_type=f32)


def far_kernel(where, hs, *refs):
    parts, (low, high), held, sems = refs[:SIDE], refs[SIDE : SIDE + 2], refs[-2], refs[-1]
    copies = []
    for k in range(SIDE):
        column = pl.multiple_of(lax.rem(where[1] + k, SIDE) * HEAD_DIM, HEAD_DIM)
        copies.append(pltpu.make_async_copy(parts[k], held.at[:, pl.ds(column, HEAD_DIM)], sems.at[k]))
    for copy in copies:
        copy.start()
    for copy in copies:
        copy.wait()
    cut = low.shape[0]
    for start in range(0, hs.shape[0], 256):
        out, at = (low, start) if start < cut else (high, start - cut)
        out[at : at + 256, :] = dot_rows(hs, held[...], start).astype(bf16)


def own_kernel(hs, weight, place, after, *refs):
    outs, held, sem = refs[:-2], refs[-2], refs[-1]
    rows = held.shape[0]
    copy = pltpu.make_async_copy(weight.at[pl.ds(pl.multiple_of(place[2] * rows, rows), rows)], held, sem)
    copy.start()
    copy.wait()
    for start in range(0, hs.shape[0], 256):
        column = 0
        for out in outs:
            width = out.shape[1]
            out[start : start + 256, :] = dot_rows(hs, held[:, column : column + width], start)
            column += width


def near_kernel(first, widths, hs, weight, far_low, far_high, *refs):
    outs = refs[-2 * len(widths) :]
    columns = far_low.shape[1]
    cut = far_low.shape[0]
    for start in range(0, hs.shape[0], 256):
        block = slice(start, start + 256)
        column = first
        for n, width in enumerate(widths):
            cols = slice(column, column + width)
            ahead = dot_rows(hs, weight[:, cols], start)
            behind = dot_rows(hs, weight[:, columns + column : columns + column + width], start)
            if start < cut:
                ahead = ahead + far_low[block, cols].astype(f32)
            else:
                behind = behind + far_high[start - cut : start - cut + 256, cols].astype(f32)
            outs[2 * n][block, :] = ahead.astype(bf16)
            outs[2 * n + 1][block, :] = behind.astype(bf16)
            column += width


def lay_pages(source, fresh, payload):
    owners, capacity = payload.shape[0], source.shape[0] // payload.shape[0]

    def place(owner, carry):
        for r in range(capacity):
            page = source[owner * capacity + r]

            @pl.when(page >= 0)
            def _():
                payload[owner, r] = fresh[pl.ds(pl.multiple_of(page * PAGE, PAGE), PAGE), :]

            @pl.when(page < 0)
            def _():
                payload[owner, r] = jnp.zeros(payload.shape[2:], bf16)

        return carry

    lax.fori_loop(0, owners, place, 0)


def sum_rows(own, ahead, behind, scale, fresh):
    for start in range(0, fresh.shape[0], 128):
        block = slice(start, start + 128)
        total = own[block, :] + ahead[block, :].astype(f32) + behind[block, :].astype(f32)
        fresh[block, :] = (total * scale[block, :1]).astype(bf16)


def keys_kernel(source, own, ahead, behind, scale, fresh, payload):
    sum_rows(own, ahead, behind, scale, fresh)
    lay_pages(source, fresh, payload)


def values_kernel(
    j, where, ends, source, own, ahead, behind, scale, keys, queries, peak, total, mixed, *refs
):
    payload, fresh = refs[-2:]
    sum_rows(own, ahead, behind, scale, fresh)
    lay_pages(source, fresh, payload)
    rows = peak.shape[0] // (keys.shape[1] // HEAD_DIM)
    count = fresh.shape[0]
    group = rows // (SESSIONS * STEPS)
    ctx = where[0] * SIDE + where[1]
    query = head_queries(queries, j, group)
    session, step, key = row_ids(rows, count)
    page = key // PAGE + ctx * (count // PAGE)
    owner_session = jnp.zeros_like(page)
    for s in range(SESSIONS):
        owner_session = owner_session + (ends[s] <= page).astype(jnp.int32)
    block = slice(j * rows, (j + 1) * rows)
    state = (peak[block, :1], total[block, :1], mixed[block, :])
    state = attend(
        state, query, keys[:, j * HEAD_DIM : (j + 1) * HEAD_DIM], fresh[...], session == owner_session
    )
    some = state[1] > 0.0
    divisor = jnp.where(some, state[1], 1.0)
    level = jnp.where(some, state[0] + jnp.log(divisor), floor_value)
    level = jnp.broadcast_to(level, (rows, HEAD_DIM))
    level = jnp.concatenate([level] * (HEAD_DIM // rows), axis=0).T[:PAGE]
    high = level.astype(bf16).astype(f32)
    middle = (level - high).astype(bf16).astype(f32)
    low = level - high - middle
    line = lax.broadcasted_iota(jnp.int32, level.shape, 0)
    terms = jnp.where(line == 0, high, jnp.where(line == 1, middle, jnp.where(line == 2, low, 0.0)))
    terms = terms.astype(bf16)
    part = (state[2] / divisor).astype(bf16).reshape(rows // PAGE, PAGE, HEAD_DIM)
    first = payload.shape[1] - rows // PAGE - 1

    def spread(owner, carry):
        payload[owner, first : first + rows // PAGE] = part
        payload[owner, first + rows // PAGE] = terms
        return carry

    lax.fori_loop(0, payload.shape[0], spread, 0)


def last_kernel(*refs):
    key_pages, value_parts, pages, out = refs[0], refs[1:-2], refs[-2], refs[-1]
    owners, capacity, _, key_cols = key_pages.shape
    for i in range(owners):
        slots = slice(i * capacity, (i + 1) * capacity)
        pages[slots, :, :key_cols] = key_pages[i]
        for j, part in enumerate(value_parts):
            column = key_cols + j * HEAD_DIM
            pages[slots, :, column : column + HEAD_DIM] = part[i, :capacity]
    steps = SESSIONS * STEPS
    for j, part in enumerate(value_parts):
        blocks = part.shape[1] - capacity - 1
        rows = blocks * PAGE
        line = lax.broadcasted_iota(jnp.int32, (owners, HEAD_DIM), 0)
        level = jnp.zeros((owners, HEAD_DIM), f32)
        for i in range(owners):
            terms = part[i, capacity + blocks].astype(f32)
            level = jnp.where(line == i, terms[0:1] + terms[1:2] + terms[2:3], level)
        share = jnp.exp(level - jnp.max(level, axis=0, keepdims=True))
        share = share / jnp.sum(share, axis=0, keepdims=True)
        share = jnp.concatenate([share, jnp.zeros((HEAD_DIM - owners, HEAD_DIM), f32)], axis=0).T
        total = jnp.zeros((rows, HEAD_DIM), f32)
        for i in range(owners):
            total = total + share[:rows, i : i + 1] * part[i, capacity : capacity + blocks].reshape(
                rows, HEAD_DIM
            ).astype(f32)
        result = total.astype(bf16)
        for g in range(rows // steps):
            column = (j * (rows // steps) + g) * HEAD_DIM
            out[:, column : column + HEAD_DIM] = result[g * steps : (g + 1) * steps, :]


def head_queries(queries, j, group):
    return jnp.concatenate(
        [queries[:, (j * group + g) * HEAD_DIM : (j * group + g + 1) * HEAD_DIM] for g in range(group)], axis=0
    )


def attend(state, query, keys, values, mask):
    peak, total, mixed = state
    scores = lax.dot_general(query, keys, (((1,), (1,)), ((), ())), preferred_element_type=f32)
    scores = jnp.where(mask, scores * HEAD_DIM ** (-0.5), floor_value)
    top = jnp.maximum(peak, jnp.max(scores, axis=1, keepdims=True))
    weights = jnp.where(mask, jnp.exp(scores - top), 0.0)
    factor = jnp.exp(peak - top)
    total = total * factor + jnp.sum(weights, axis=1, keepdims=True)
    mixed = mixed * factor + jnp.dot(weights.astype(bf16), values, preferred_element_type=f32)
    return top, total, mixed


def row_ids(rows, length):
    row = lax.broadcasted_iota(jnp.int32, (rows, length), 0) % (SESSIONS * STEPS)
    key = lax.broadcasted_iota(jnp.int32, (rows, length), 1)
    return row // STEPS, row % STEPS, key


def cache_kernel(where, lengths, queries, cache, new, after, peak_out, total_out, mixed_out):
    per_group = cache.shape[2] // (2 * HEAD_DIM)
    group = queries.shape[1] // (HEAD_DIM * per_group)
    rows = group * SESSIONS * STEPS
    local = cache.shape[1]
    ctx = where[0] * SIDE + where[1]
    for j in range(per_group):
        query = head_queries(queries, j, group)
        key_cols = slice(j * HEAD_DIM, (j + 1) * HEAD_DIM)
        value_cols = slice((per_group + j) * HEAD_DIM, (per_group + j + 1) * HEAD_DIM)
        state = (
            jnp.full((rows, 1), floor_value, f32),
            jnp.zeros((rows, 1), f32),
            jnp.zeros((rows, HEAD_DIM), f32),
        )
        for s in range(SESSIONS):
            session, step, key = row_ids(rows, local)
            mask = (session == s) & (key + ctx * local < lengths[s])
            state = attend(state, query, cache[s, :, key_cols], cache[s, :, value_cols], mask)
        session, step, key = row_ids(rows, new.shape[0])
        mask = (session == key // STEPS) & (key % STEPS <= step) & (ctx == 0)
        state = attend(state, query, new[:, key_cols], new[:, value_cols], mask)
        block = slice(j * rows, (j + 1) * rows)
        peak_out[block, :] = jnp.broadcast_to(state[0], (rows, HEAD_DIM))
        total_out[block, :] = jnp.broadcast_to(state[1], (rows, HEAD_DIM))
        mixed_out[block, :] = state[2]


def call(kernel, out_shape, in_specs, *operands, vmem=16, scratch=()):
    return pl.pallas_call(
        kernel,
        out_shape=out_shape,
        in_specs=in_specs,
        out_specs=jax.tree.map(lambda _: VMEM, out_shape),
        scratch_shapes=scratch,
        compiler_params=pltpu.CompilerParams(vmem_limit_bytes=vmem * MEBI),
        cost_estimate=NO_COST,
    )(*operands)


def per_device(
    layer_inputs, norm_gain, kv_weight, span_pages, page_owner, cache_len, cache_kv, queries, new_kv
):
    n_ctx = lax.axis_size("ctx")
    ctx_index = lax.axis_index("ctx")
    tp_index = lax.axis_index("tp")
    place = jnp.stack([ctx_index // SIDE, ctx_index % SIDE, tp_index]).astype(jnp.int32)
    own_part = layer_inputs[0]
    row_count, features = own_part.shape
    weight = kv_weight[0]
    kv_cols = weight.shape[1]
    shape = jax.ShapeDtypeStruct

    part_rows = features // SIDE
    one, three, band = call(
        pieces_kernel,
        [shape((part_rows, HEAD_DIM), bf16)] * 3,
        [SMEM, ANY],
        place,
        weight,
        scratch=[pltpu.SemaphoreType.DMA((3,))],
    )
    band = shift_tp(band, 2)
    near = jnp.stack([shift_tp(one, -1), shift_tp(three, 1)])
    far_column = call(
        functools.partial(rows_kernel, 0),
        shape((features, HEAD_DIM), bf16),
        [SMEM] + [VMEM] * SIDE,
        place,
        band,
        *[from_x(band, k) for k in range(1, SIDE)],
    )
    near_column = call(
        functools.partial(rows_kernel, 1),
        shape((2, features, HEAD_DIM), bf16),
        [SMEM] + [VMEM] * SIDE,
        place,
        near,
        *[from_y(near, k) for k in range(1, SIDE)],
    )
    far_parts = [far_column] + [from_y(far_column, k) for k in range(1, SIDE)]
    near_weight = call(
        columns_kernel,
        shape((features, 2 * kv_cols), bf16),
        [SMEM] + [VMEM] * SIDE,
        place,
        near_column,
        *[from_x(near_column, k) for k in range(1, SIDE)],
    )

    inner = lax.ppermute(own_part, "section", [(0, 1), (2, 3)])
    crossed = lax.ppermute(add_after(inner, own_part, band, near), "section", [(1, 2)])
    crossed = tied(crossed, near_column, *far_parts)
    passed = lax.ppermute(crossed, "section", [(2, 3)])

    arrived = (inner.astype(f32) + crossed.astype(f32) + passed.astype(f32)).astype(bf16)
    hidden = added(arrived, own_part)
    wide = hidden.astype(f32)
    hs = (wide * norm_gain[0].astype(f32)).astype(bf16)
    squares = jnp.sum(wide * wide, axis=1).reshape(-1, HEAD_DIM)

    cut = row_count // 2
    far_low, far_high = call(
        far_kernel,
        [shape((cut, kv_cols), bf16), shape((row_count - cut, kv_cols), bf16)],
        [SMEM, VMEM] + [ANY] * SIDE,
        place,
        hs,
        *far_parts,
        scratch=[pltpu.VMEM((features, kv_cols), bf16), pltpu.SemaphoreType.DMA((SIDE,))],
    )
    key_cols = kv_cols // 2
    value_cols = [HEAD_DIM] * (key_cols // HEAD_DIM)
    own = call(
        own_kernel,
        [shape((row_count, width), f32) for width in [key_cols] + value_cols],
        [VMEM, ANY, SMEM, ANY],
        hs,
        weight,
        place,
        far_low,
        scratch=[pltpu.VMEM((features, kv_cols), bf16), pltpu.SemaphoreType.DMA],
    )
    squares = squares + shift_tp(squares, 1) + shift_tp(squares, -1) + shift_tp(squares, 2)
    scale = jnp.broadcast_to(
        lax.rsqrt(squares / D + epsilon).reshape(row_count, 1), (row_count, HEAD_DIM)
    )
    query = queries[0].reshape(SESSIONS * STEPS, -1)
    new = jnp.pad(new_kv[0].reshape(SESSIONS * STEPS, kv_cols), ((0, HEAD_DIM - SESSIONS * STEPS), (0, 0)))
    state_shape = shape((query.shape[1] // HEAD_DIM * SESSIONS * STEPS, HEAD_DIM), f32)
    state = call(
        cache_kernel,
        [state_shape] * 3,
        [SMEM, SMEM, VMEM, VMEM, VMEM, ANY],
        place,
        cache_len,
        query,
        cache_kv[0],
        new,
        far_low,
    )
    passing = (shift_tp(far_low, 1), shift_tp(far_high, -1))
    key_sums = call(
        functools.partial(near_kernel, 0, [key_cols]),
        [shape((row_count, key_cols), bf16)] * 2,
        [VMEM] * 4 + [ANY] * 4,
        hs,
        near_weight,
        *passing,
        *state,
        own[0],
    )
    value_sums = call(
        functools.partial(near_kernel, key_cols, value_cols),
        [shape((row_count, HEAD_DIM), bf16)] * (2 * len(value_cols)),
        [VMEM] * 4 + [ANY],
        hs,
        near_weight,
        *passing,
        key_sums[0],
    )
    key_sums = (shift_tp(key_sums[0], 1), shift_tp(key_sums[1], -1))
    value_sums = [shift_tp(part, 1 if n % 2 == 0 else -1) for n, part in enumerate(value_sums)]

    pages_dev = row_count // PAGE
    capacity = max(2, 2 * pages_dev // n_ctx)
    owner = lax.dynamic_slice_in_dim(page_owner[:, 0], ctx_index * pages_dev, pages_dev)
    order = jnp.arange(pages_dev, dtype=jnp.int32)
    earlier = (owner[:, None] == owner[None, :]) & (order[None, :] < order[:, None])
    target = owner * capacity + jnp.sum(earlier.astype(jnp.int32), axis=1)
    slots = jnp.arange(n_ctx * capacity, dtype=jnp.int32)
    source = jnp.max(jnp.where(target[None, :] == slots[:, None], order[None, :], -1), axis=1)
    ends = jnp.cumsum(span_pages)

    fresh_keys, key_pages = call(
        keys_kernel,
        [shape((row_count, key_cols), bf16), shape((n_ctx, capacity, PAGE, key_cols), bf16)],
        [SMEM] + [VMEM] * 4,
        source,
        own[0],
        *key_sums,
        scale,
    )
    key_pages = lax.all_to_all(key_pages, "ctx", split_axis=0, concat_axis=0, tiled=True)
    value_parts = []
    for j in range(len(value_cols)):
        rows = state_shape.shape[0] // len(value_cols)
        payload = call(
            functools.partial(values_kernel, j),
            shape((n_ctx, capacity + rows // PAGE + 1, PAGE, HEAD_DIM), bf16),
            [SMEM] * 3 + [VMEM] * 9 + [ANY] * j,
            place,
            ends,
            source,
            own[1 + j],
            value_sums[2 * j],
            value_sums[2 * j + 1],
            scale,
            fresh_keys,
            query,
            *state,
            *[key_pages] * j,
            scratch=[pltpu.VMEM((row_count, HEAD_DIM), bf16)],
        )
        value_parts.append(lax.all_to_all(payload, "ctx", split_axis=0, concat_axis=0, tiled=True))
    page_store, attention = call(
        last_kernel,
        [shape((n_ctx * capacity, PAGE, kv_cols), bf16), shape(query.shape, bf16)],
        [VMEM] * (1 + len(value_parts)),
        key_pages,
        *value_parts,
    )
    return (page_store[None], attention.reshape(1, SESSIONS, STEPS, -1))


def solution(mesh):
    return jax.shard_map(
        per_device,
        mesh=mesh,
        in_specs=(
            P("section", "ctx", "tp"),
            P("section", "tp"),
            P("section", None, "tp"),
            P(),
            P(),
            P(),
            P("section", None, "ctx", "tp"),
            P("section", None, None, "tp"),
            P("section", None, None, "tp"),
        ),
        out_specs=(P("section", "ctx", None, "tp"), P("section", None, None, "tp")),
        check_vma=False,
    )
```

```python
import functools

import jax
import jax.numpy as jnp
from jax import lax
from jax.experimental import pallas as pl
from jax.experimental.pallas import tpu as pltpu
from jax.sharding import PartitionSpec as P

D = 5120
HEAD_DIM = 128
SESSIONS = 4
STEPS = 4
PAGE = 16
SIDE = 4

epsilon = 1e-05
floor_value = -1e30
bf16 = jnp.bfloat16
f32 = jnp.float32
TOKEN = jax.ShapeDtypeStruct((8, HEAD_DIM), jnp.float32)
VMEM = pl.BlockSpec(memory_space=pltpu.VMEM)
SMEM = pl.BlockSpec(memory_space=pltpu.SMEM)
ANY = pl.BlockSpec(memory_space=pl.ANY)
HBM = pl.BlockSpec(memory_space=pltpu.HBM)
MEBI = 1024 * 1024
SOME_COST = pl.CostEstimate(flops=8_000_000_000, bytes_accessed=0, transcendentals=0)
NO_COST = pl.CostEstimate(flops=0, bytes_accessed=0, transcendentals=0)


def shift_tp(array, by):
    peers = lax.axis_size("tp")
    return lax.ppermute(array, "tp", [(i, (i + by) % peers) for i in range(peers)])


def from_x(array, by):
    pairs = [(((i // SIDE + by) % SIDE) * SIDE + i % SIDE, i) for i in range(SIDE * SIDE)]
    return lax.ppermute(array, "ctx", pairs)


def from_y(array, by):
    pairs = [((i // SIDE) * SIDE + (i % SIDE + by) % SIDE, i) for i in range(SIDE * SIDE)]
    return lax.ppermute(array, "ctx", pairs)


def added(first, second):
    return (first.astype(f32) + second.astype(f32)).astype(bf16)


def add_kernel(first, second, *refs):
    refs[-1][...] = added(first[...], second[...])


def add_after(first, second, *after):
    rows, columns = first.shape
    block = pl.BlockSpec((rows // 4, columns), lambda i: (i, 0))
    return pl.pallas_call(
        add_kernel,
        grid=(4,),
        out_shape=jax.ShapeDtypeStruct(first.shape, bf16),
        in_specs=[block, block] + [VMEM] * len(after),
        out_specs=block,
        compiler_params=pltpu.CompilerParams(vmem_limit_bytes=8 * MEBI),
        cost_estimate=SOME_COST,
    )(first, second, *after)


def token_kernel(*refs):
    refs[-1][...] = jnp.zeros(refs[-1].shape, refs[-1].dtype)


def nothing(*refs):
    pass


def tied(array, *after):
    return pl.pallas_call(
        nothing,
        out_shape=jax.ShapeDtypeStruct(array.shape, array.dtype),
        in_specs=[VMEM] * (1 + len(after)),
        out_specs=VMEM,
        input_output_aliases={0: 0},
        compiler_params=pltpu.CompilerParams(vmem_limit_bytes=8 * MEBI),
        cost_estimate=NO_COST,
    )(array, *after)


def tied_pair(first, second, *after):
    shapes = [jax.ShapeDtypeStruct(a.shape, a.dtype) for a in (first, second)]
    return pl.pallas_call(
        nothing,
        out_shape=shapes,
        in_specs=[VMEM] * (2 + len(after)),
        out_specs=[VMEM, VMEM],
        input_output_aliases={0: 0, 1: 1},
        compiler_params=pltpu.CompilerParams(vmem_limit_bytes=8 * MEBI),
        cost_estimate=NO_COST,
    )(first, second, *after)


def pieces_kernel(place, weight, one, three, far, sems):
    x, y, rank = place[0], place[1], place[2]
    rows = one.shape[0]
    features = rows * SIDE
    copies = []
    for n, (out, behind, row, column) in enumerate(((one, 1, y, x), (three, 3, y, x), (far, 2, x, y))):
        start = lax.rem(rank + SIDE - behind, SIDE) * features + row * rows
        copies.append(
            pltpu.make_async_copy(
                weight.at[
                    pl.ds(pl.multiple_of(start, rows), rows),
                    pl.ds(pl.multiple_of(column * HEAD_DIM, HEAD_DIM), HEAD_DIM),
                ],
                out,
                sems.at[n],
            )
        )
    for copy in copies:
        copy.start()
    for copy in copies:
        copy.wait()


def rows_kernel(axis, place, *refs):
    out, token = refs[-2:]
    rows = refs[0].shape[-2]
    for k in range(SIDE):
        start = pl.multiple_of(lax.rem(place[axis] + k, SIDE) * rows, rows)
        if len(out.shape) == 2:
            out[pl.ds(start, rows), :] = refs[k][...]
        else:
            out[:, pl.ds(start, rows), :] = refs[k][...]
    token[...] = jnp.zeros(token.shape, token.dtype)


def columns_kernel(place, *refs):
    out = refs[-1]
    half = out.shape[1] // 2
    for k in range(SIDE):
        start = lax.rem(place[0] + k, SIDE) * HEAD_DIM
        for n in range(2):
            out[:, pl.ds(pl.multiple_of(n * half + start, HEAD_DIM), HEAD_DIM)] = refs[k][n]


def dot_rows(hs, weight, start):
    return jnp.dot(hs[start : start + 256, :], weight, preferred_element_type=f32)


def to_terms(sums, width):
    high = sums.astype(bf16).astype(f32)
    middle = (sums - high).astype(bf16).astype(f32)
    low = sums - high - middle
    blank = jnp.zeros(sums.shape, f32)
    pad = [jnp.zeros((16, width - 2 * HEAD_DIM), f32)] if width > 2 * HEAD_DIM else []
    first = jnp.concatenate([high, low], axis=0)
    second = jnp.concatenate([middle, blank], axis=0)
    return jnp.concatenate([first, second] + pad, axis=1).astype(bf16)


def from_terms(rows):
    rows = rows.astype(f32)
    return rows[:8, :HEAD_DIM] + rows[:8, HEAD_DIM : 2 * HEAD_DIM] + rows[8:, :HEAD_DIM]


def far_kernel(where, squares, hs, *refs):
    parts, (low, high, token), held, sems = refs[:SIDE], refs[SIDE : SIDE + 3], refs[-2], refs[-1]
    token[...] = jnp.zeros(token.shape, token.dtype)
    copies = []
    for k in range(SIDE):
        column = pl.multiple_of(lax.rem(where[1] + k, SIDE) * HEAD_DIM, HEAD_DIM)
        copies.append(pltpu.make_async_copy(parts[k], held.at[:, pl.ds(column, HEAD_DIM)], sems.at[k]))
    for copy in copies:
        copy.start()
    for copy in copies:
        copy.wait()
    cut = hs.shape[0] - high.shape[0]
    for start in range(0, hs.shape[0], 256):
        out, at = (low, start) if start < cut else (high, start - cut)
        out[at : at + 256, :] = dot_rows(hs, held[...], start).astype(bf16)
    low[cut:, :] = to_terms(squares[...], low.shape[1])


def hidden_kernel(info, chip, crossed, passed, gain, hs, squares):
    step = pl.program_id(0)
    groups = hs.shape[0] // HEAD_DIM

    @pl.when(step == 0)
    def _():
        squares[...] = jnp.zeros(squares.shape, f32)

    wide = chip[...].astype(f32) + crossed[...].astype(f32) + passed[...].astype(f32)
    wide = wide.astype(bf16).astype(f32)
    hs[...] = (wide * gain[...].astype(f32)).astype(bf16)
    sums = jnp.sum(wide * wide, axis=1, keepdims=True)
    line = lax.broadcasted_iota(jnp.int32, squares.shape, 0)
    for n in range(groups):
        turned = jnp.broadcast_to(sums[n * HEAD_DIM : (n + 1) * HEAD_DIM], (HEAD_DIM, HEAD_DIM)).T[:8]
        squares[...] = jnp.where(line == step * groups + n, turned, squares[...])


def hidden_state(info, chip, crossed, passed, gain):
    rows, features = chip.shape
    block = rows // 4

    def wanted(*sections):
        def index(i, info):
            needed = functools.reduce(jnp.logical_or, [info[3] == s for s in sections])
            return jnp.where(needed, i, 0), 0

        return pl.BlockSpec((block, features), index)

    return pl.pallas_call(
        hidden_kernel,
        grid_spec=pltpu.PrefetchScalarGridSpec(
            num_scalar_prefetch=1,
            grid=(4,),
            in_specs=[
                wanted(0, 1, 2, 3),
                wanted(2),
                wanted(3),
                pl.BlockSpec((1, features), lambda i, info: (0, 0)),
            ],
            out_specs=[
                pl.BlockSpec((block, features), lambda i, info: (i, 0)),
                pl.BlockSpec((8, HEAD_DIM), lambda i, info: (0, 0)),
            ],
        ),
        out_shape=[jax.ShapeDtypeStruct((rows, features), bf16), TOKEN],
        compiler_params=pltpu.CompilerParams(vmem_limit_bytes=16 * MEBI),
        cost_estimate=SOME_COST,
    )(info, chip, crossed, passed, gain)


def own_kernel(hs, weight, place, after, *refs):
    outs, token, held, sem = refs[:-3], refs[-3], refs[-2], refs[-1]
    token[...] = jnp.zeros(token.shape, token.dtype)
    rows = held.shape[0]
    copy = pltpu.make_async_copy(weight.at[pl.ds(pl.multiple_of(place[2] * rows, rows), rows)], held, sem)
    copy.start()
    copy.wait()
    for start in range(0, hs.shape[0], 256):
        column = 0
        for out in outs:
            width = out.shape[1]
            out[start : start + 256, :] = dot_rows(hs, held[:, column : column + width], start)
            column += width


def near_kernel(widths, squares, hs, weight, far_low, far_high, *refs):
    outs, token = refs[:-1], refs[-1]
    token[...] = jnp.zeros(token.shape, token.dtype)
    rows = hs.shape[0]
    columns = far_low.shape[1]
    cut = rows - far_high.shape[0]
    column = 0
    for n, width in enumerate(widths):
        cols = slice(column, column + width)
        for start in range(0, rows, 256):
            block = slice(start, start + 256)
            ahead = dot_rows(hs, weight[:, cols], start)
            behind = dot_rows(hs, weight[:, columns + column : columns + column + width], start)
            if start < cut:
                ahead = ahead + far_low[block, cols].astype(f32)
            else:
                behind = behind + far_high[start - cut : start - cut + 256, cols].astype(f32)
            outs[2 * n][block, :] = ahead.astype(bf16)
            outs[2 * n + 1][block, :] = behind.astype(bf16)
        column += width
    width = widths[0]
    outs[0][rows:, :] = to_terms(squares[...] + from_terms(far_low[cut:, :]), width)
    outs[1][rows:, :] = to_terms(squares[...], width)


def lay_pages(source, fresh, payload):
    owners, capacity = payload.shape[0], source.shape[0] // payload.shape[0]

    def place(owner, carry):
        for r in range(capacity):
            page = source[owner * capacity + r]
            payload[owner, r] = fresh[pl.ds(pl.multiple_of(page * PAGE, PAGE), PAGE), :]
        return carry

    lax.fori_loop(0, owners, place, 0)


def sum_rows(own, ahead, behind, scale, fresh):
    for n in range(own.shape[0] // HEAD_DIM):
        block = slice(n * HEAD_DIM, (n + 1) * HEAD_DIM)
        factor = jnp.broadcast_to(scale[n : n + 1, :], (HEAD_DIM, HEAD_DIM)).T[:, :1]
        total = own[block, :] + ahead[block, :].astype(f32) + behind[block, :].astype(f32)
        fresh[block, :] = (total * factor).astype(bf16)
    fresh[own.shape[0] :, :] = jnp.zeros((PAGE, fresh.shape[1]), bf16)


def keys_kernel(
    heads, place, ends, source, squares, own, ahead, behind, queries, peak, total, mixed, *refs
):
    scale, fresh, payload, weights_out, level_out, mixed_out = refs
    rows = own.shape[0]
    sums = squares[...] + from_terms(ahead[rows:, :]) + from_terms(behind[rows:, :])
    scale[...] = lax.rsqrt(sums / D + epsilon)
    sum_rows(own, ahead, behind, scale, fresh)
    lay_pages(source, fresh, payload)
    lines = peak.shape[0] // heads
    group = lines // (SESSIONS * STEPS)
    ctx = place[0] * SIDE + place[1]
    session, step, key = row_ids(lines, rows)
    page = key // PAGE + ctx * (rows // PAGE)
    owner_session = jnp.zeros_like(page)
    for s in range(SESSIONS):
        owner_session = owner_session + (ends[s] <= page).astype(jnp.int32)
    mask = session == owner_session
    for j in range(heads):
        block = slice(j * lines, (j + 1) * lines)
        query = head_queries(queries, j, group)
        scores = lax.dot_general(
            query,
            fresh[:rows, j * HEAD_DIM : (j + 1) * HEAD_DIM],
            (((1,), (1,)), ((), ())),
            preferred_element_type=f32,
        )
        scores = jnp.where(mask, scores * HEAD_DIM ** (-0.5), floor_value)
        old = peak[block, :1]
        top = jnp.maximum(old, jnp.max(scores, axis=1, keepdims=True))
        weights = jnp.where(mask, jnp.exp(scores - top), 0.0)
        factor = jnp.exp(old - top)
        amount = total[block, :1] * factor + jnp.sum(weights, axis=1, keepdims=True)
        some = amount > 0.0
        divisor = jnp.where(some, amount, 1.0)
        weights_out[block, :] = weights.astype(bf16)
        level = jnp.where(some, top + jnp.log(divisor), floor_value)
        level_out[block, :] = jnp.broadcast_to(level, (lines, HEAD_DIM))
        mixed_out[block, :HEAD_DIM] = mixed[block, :] * factor
        mixed_out[block, HEAD_DIM:] = jnp.broadcast_to(1.0 / divisor, (lines, HEAD_DIM))


def values_kernel(heads, source, own, ahead, behind, scale, weights, levels, mixed, payload, fresh):
    sum_rows(own, ahead, behind, scale, fresh)
    lay_pages(source, fresh, payload)
    lines = weights.shape[0] // heads
    parts = []
    for j in range(heads):
        block = slice(j * lines, (j + 1) * lines)
        cols = slice(j * HEAD_DIM, (j + 1) * HEAD_DIM)
        part = mixed[block, :HEAD_DIM] + jnp.dot(
            weights[block, :], fresh[: own.shape[0], cols], preferred_element_type=f32
        )
        part = part * mixed[block, HEAD_DIM:]
        parts.append(part.astype(bf16).reshape(lines // PAGE, PAGE, HEAD_DIM))
    level = levels[...].T[:PAGE]
    high = level.astype(bf16).astype(f32)
    middle = (level - high).astype(bf16).astype(f32)
    low = level - high - middle
    line = lax.broadcasted_iota(jnp.int32, level.shape, 0)
    terms = jnp.where(line == 0, high, jnp.where(line == 1, middle, jnp.where(line == 2, low, 0.0)))
    terms = terms.astype(bf16)
    last = payload.shape[1] - 1
    first = last - lines // PAGE

    def spread(owner, carry):
        for j in range(heads):
            payload[owner, first:last, :, j * HEAD_DIM : (j + 1) * HEAD_DIM] = parts[j]
        payload[owner, last, :, :HEAD_DIM] = terms
        payload[owner, last, :, HEAD_DIM:] = jnp.zeros_like(payload[owner, last, :, HEAD_DIM:])
        return carry

    lax.fori_loop(0, payload.shape[0], spread, 0)


def last_kernel(key_pages, value_part, pages, out):
    owners, capacity, _, key_cols = key_pages.shape
    for i in range(owners):
        slots = slice(i * capacity, (i + 1) * capacity)
        pages[slots, :, :key_cols] = key_pages[i]
        pages[slots, :, key_cols:] = value_part[i, :capacity]
    steps = SESSIONS * STEPS
    heads = key_cols // HEAD_DIM
    last = value_part.shape[1] - 1
    rows = (last - capacity) * PAGE
    line = lax.broadcasted_iota(jnp.int32, (owners, HEAD_DIM), 0)
    level = jnp.zeros((owners, HEAD_DIM), f32)
    for i in range(owners):
        terms = value_part[i, last, :, :HEAD_DIM].astype(f32)
        level = jnp.where(line == i, terms[0:1] + terms[1:2] + terms[2:3], level)
    share = jnp.exp(level - jnp.max(level, axis=0, keepdims=True))
    share = share / jnp.sum(share, axis=0, keepdims=True)
    share = jnp.concatenate([share, jnp.zeros((HEAD_DIM - owners, HEAD_DIM), f32)], axis=0).T
    for j in range(heads):
        total = jnp.zeros((rows, HEAD_DIM), f32)
        for i in range(owners):
            part = value_part[i, capacity:last, :, j * HEAD_DIM : (j + 1) * HEAD_DIM]
            total = total + share[j * rows : (j + 1) * rows, i : i + 1] * part.reshape(rows, HEAD_DIM).astype(f32)
        result = total.astype(bf16)
        for g in range(rows // steps):
            column = (j * (rows // steps) + g) * HEAD_DIM
            out[:, column : column + HEAD_DIM] = result[g * steps : (g + 1) * steps, :]


def head_queries(queries, j, group):
    return jnp.concatenate(
        [queries[:, (j * group + g) * HEAD_DIM : (j * group + g + 1) * HEAD_DIM] for g in range(group)], axis=0
    )


def attend(state, query, keys, values, mask):
    peak, total, mixed = state
    scores = lax.dot_general(query, keys, (((1,), (1,)), ((), ())), preferred_element_type=f32)
    scores = jnp.where(mask, scores * HEAD_DIM ** (-0.5), floor_value)
    top = jnp.maximum(peak, jnp.max(scores, axis=1, keepdims=True))
    weights = jnp.where(mask, jnp.exp(scores - top), 0.0)
    factor = jnp.exp(peak - top)
    total = total * factor + jnp.sum(weights, axis=1, keepdims=True)
    mixed = mixed * factor + jnp.dot(weights.astype(bf16), values, preferred_element_type=f32)
    return top, total, mixed


def row_ids(rows, length):
    row = lax.broadcasted_iota(jnp.int32, (rows, length), 0) % (SESSIONS * STEPS)
    key = lax.broadcasted_iota(jnp.int32, (rows, length), 1)
    return row // STEPS, row % STEPS, key


def cache_kernel(where, lengths, early, queries, cache, new, after, peak_out, total_out, mixed_out):
    per_group = cache.shape[2] // (2 * HEAD_DIM)
    group = queries.shape[1] // (HEAD_DIM * per_group)
    rows = group * SESSIONS * STEPS
    local = cache.shape[1]
    ctx = where[0] * SIDE + where[1]
    for j in range(per_group):
        query = head_queries(queries, j, group)
        key_cols = slice(j * HEAD_DIM, (j + 1) * HEAD_DIM)
        value_cols = slice((per_group + j) * HEAD_DIM, (per_group + j + 1) * HEAD_DIM)
        state = (
            jnp.full((rows, 1), floor_value, f32),
            jnp.zeros((rows, 1), f32),
            jnp.zeros((rows, HEAD_DIM), f32),
        )
        for s in range(SESSIONS):
            session, step, key = row_ids(rows, local)
            mask = (session == s) & (key + ctx * local < lengths[s])
            state = attend(state, query, cache[s, :, key_cols], cache[s, :, value_cols], mask)
        session, step, key = row_ids(rows, new.shape[0])
        mask = (session == key // STEPS) & (key % STEPS <= step) & (ctx == 0)
        state = attend(state, query, new[:, key_cols], new[:, value_cols], mask)
        block = slice(j * rows, (j + 1) * rows)
        peak_out[block, :] = jnp.broadcast_to(state[0], (rows, HEAD_DIM))
        total_out[block, :] = jnp.broadcast_to(state[1], (rows, HEAD_DIM))
        mixed_out[block, :] = state[2]


def call(kernel, out_shape, in_specs, *operands, vmem=16, scratch=(), cost=NO_COST):
    return pl.pallas_call(
        kernel,
        out_shape=out_shape,
        in_specs=in_specs,
        out_specs=jax.tree.map(lambda _: VMEM, out_shape),
        scratch_shapes=scratch,
        compiler_params=pltpu.CompilerParams(vmem_limit_bytes=vmem * MEBI),
        cost_estimate=cost,
    )(*operands)


def per_device(
    layer_inputs, norm_gain, kv_weight, span_pages, page_owner, cache_len, cache_kv, queries, new_kv
):
    n_ctx = lax.axis_size("ctx")
    ctx_index = lax.axis_index("ctx")
    tp_index = lax.axis_index("tp")
    place = jnp.stack([ctx_index // SIDE, ctx_index % SIDE, tp_index]).astype(jnp.int32)
    own_part = layer_inputs[0]
    row_count, features = own_part.shape
    weight = kv_weight[0]
    kv_cols = weight.shape[1]
    shape = jax.ShapeDtypeStruct

    part_rows = features // SIDE
    one, three, band = call(
        pieces_kernel,
        [shape((part_rows, HEAD_DIM), bf16)] * 3,
        [SMEM, HBM],
        place,
        weight,
        scratch=[pltpu.SemaphoreType.DMA((3,))],
        cost=SOME_COST,
    )
    band = shift_tp(band, 2)
    near = jnp.stack([shift_tp(one, -1), shift_tp(three, 1)])
    pages_dev = row_count // PAGE
    capacity = max(2, 2 * pages_dev // n_ctx)
    owner = lax.dynamic_slice_in_dim(page_owner[:, 0], ctx_index * pages_dev, pages_dev)
    order = jnp.arange(pages_dev, dtype=jnp.int32)
    earlier = (owner[:, None] == owner[None, :]) & (order[None, :] < order[:, None])
    target = owner * capacity + jnp.sum(earlier.astype(jnp.int32), axis=1)
    slots = jnp.arange(n_ctx * capacity, dtype=jnp.int32)
    source = jnp.max(jnp.where(target[None, :] == slots[:, None], order[None, :], -1), axis=1)
    source = jnp.where(source < 0, pages_dev, source)
    ends = jnp.cumsum(span_pages)

    query = queries[0].reshape(SESSIONS * STEPS, -1)
    new = jnp.pad(new_kv[0].reshape(SESSIONS * STEPS, kv_cols), ((0, HEAD_DIM - SESSIONS * STEPS), (0, 0)))
    state_shape = shape((query.shape[1] // HEAD_DIM * SESSIONS * STEPS, HEAD_DIM), f32)

    band_x = [from_x(band, k) for k in range(1, SIDE)]
    near_y = [from_y(near, k) for k in range(1, SIDE)]
    far_column, gathered = call(
        functools.partial(rows_kernel, 0),
        [shape((features, HEAD_DIM), bf16), TOKEN],
        [SMEM] + [VMEM] * (2 * SIDE - 1),
        place,
        band,
        *band_x,
        *near_y,
    )
    near_column, _ = call(
        functools.partial(rows_kernel, 1),
        [shape((2, features, HEAD_DIM), bf16), TOKEN],
        [SMEM] + [VMEM] * SIDE,
        place,
        near,
        *near_y,
    )
    far_parts = [far_column] + [from_y(far_column, k) for k in range(1, SIDE)]
    state = call(
        cache_kernel,
        [state_shape] * 3,
        [SMEM, SMEM, SMEM, VMEM, VMEM, VMEM, VMEM],
        place,
        cache_len,
        source,
        query,
        cache_kv[0],
        new,
        gathered,
    )
    near_x = [from_x(near_column, k) for k in range(1, SIDE)]

    inner = lax.ppermute(own_part, "section", [(0, 1), (2, 3)])
    chip = add_after(inner, own_part, band, near)
    crossed = lax.ppermute(chip, "section", [(1, 2)])
    crossed = tied(crossed, state[0], near_column, *far_parts)
    passed = lax.ppermute(crossed, "section", [(2, 3)])

    info = jnp.concatenate([place, lax.axis_index("section").astype(jnp.int32)[None]])
    hs, squares = hidden_state(info, chip, crossed, passed, norm_gain)

    cut = row_count // 2
    far_low, far_high, far_done = call(
        far_kernel,
        [shape((cut + 16, kv_cols), bf16), shape((row_count - cut, kv_cols), bf16), TOKEN],
        [SMEM, VMEM, VMEM] + [VMEM] * SIDE,
        place,
        squares,
        hs,
        *far_parts,
        scratch=[pltpu.VMEM((features, kv_cols), bf16), pltpu.SemaphoreType.DMA((SIDE,))],
    )
    key_cols = kv_cols // 2
    own = call(
        own_kernel,
        [shape((row_count, width), f32) for width in (key_cols, kv_cols - key_cols)] + [TOKEN],
        [VMEM, HBM, SMEM, VMEM],
        hs,
        weight,
        place,
        far_done,
        scratch=[pltpu.VMEM((features, kv_cols), bf16), pltpu.SemaphoreType.DMA],
    )
    near_weight = call(
        columns_kernel,
        shape((features, 2 * kv_cols), bf16),
        [SMEM] + [VMEM] * (SIDE + 1),
        place,
        near_column,
        *near_x,
        own[2],
    )
    passing = (shift_tp(far_low, 1), shift_tp(far_high, -1))
    ahead, behind, ahead_values, behind_values, near_done = call(
        functools.partial(near_kernel, [key_cols, kv_cols - key_cols]),
        [shape((row_count + 16, key_cols), bf16)] * 2
        + [shape((row_count, kv_cols - key_cols), bf16)] * 2
        + [TOKEN],
        [VMEM] * 5,
        squares,
        hs,
        near_weight,
        *passing,
        vmem=24,
    )
    key_sums = (shift_tp(ahead, 1), shift_tp(behind, -1))
    token = call(token_kernel, TOKEN, [VMEM] * 2, *key_sums)
    token = lax.ppermute(token, "section", [(0, 1), (1, 0), (2, 3), (3, 2)])
    ahead, behind = tied_pair(ahead_values, behind_values, token)
    value_sums = (shift_tp(ahead, 1), shift_tp(behind, -1))

    heads = key_cols // HEAD_DIM
    state_rows = state_shape.shape[0]

    def send_keys(squares, own_keys, ahead, behind, state):
        scale, fresh, pages, weights, levels, mixed = call(
            functools.partial(keys_kernel, heads),
            [
                TOKEN,
                shape((row_count + PAGE, key_cols), bf16),
                shape((n_ctx, capacity, PAGE, key_cols), bf16),
                shape((state_rows, row_count), bf16),
                state_shape,
                shape((state_rows, 2 * HEAD_DIM), f32),
            ],
            [SMEM] * 3 + [VMEM] * 8,
            place,
            ends,
            source,
            squares,
            own_keys,
            ahead,
            behind,
            query,
            *state,
        )
        pages = lax.all_to_all(pages, "ctx", split_axis=0, concat_axis=0, tiled=True)
        return pages, scale, weights, levels, mixed

    def send_none(squares, own_keys, ahead, behind, state):
        return (
            jnp.zeros((n_ctx, capacity, PAGE, key_cols), bf16),
            squares,
            jnp.zeros((state_rows, row_count), bf16),
            state[0],
            jnp.zeros((state_rows, 2 * HEAD_DIM), f32),
        )

    key_pages, scale, weights, levels, mixed = lax.cond(
        span_pages[0] >= 0, send_keys, send_none, squares, own[0], *key_sums, state
    )
    payload = call(
        functools.partial(values_kernel, heads),
        shape((n_ctx, capacity + state_rows // heads // PAGE + 1, PAGE, kv_cols - key_cols), bf16),
        [SMEM] + [VMEM] * 7,
        source,
        own[1],
        *value_sums,
        scale,
        weights,
        levels,
        mixed,
        scratch=[pltpu.VMEM((row_count + PAGE, kv_cols - key_cols), bf16)],
    )
    value_part = lax.all_to_all(payload, "ctx", split_axis=0, concat_axis=0, tiled=True)
    page_store, attention = call(
        last_kernel,
        [shape((n_ctx * capacity, PAGE, kv_cols), bf16), shape(query.shape, bf16)],
        [VMEM] * 2,
        key_pages,
        value_part,
    )
    return (page_store[None], attention.reshape(1, SESSIONS, STEPS, -1))


def solution(mesh):
    return jax.shard_map(
        per_device,
        mesh=mesh,
        in_specs=(
            P("section", "ctx", "tp"),
            P("section", "tp"),
            P("section", None, "tp"),
            P(),
            P(),
            P(),
            P("section", None, "ctx", "tp"),
            P("section", None, None, "tp"),
            P("section", None, None, "tp"),
        ),
        out_specs=(P("section", "ctx", None, "tp"), P("section", None, None, "tp")),
        check_vma=False,
    )
```
